32 devices in a mesh: grp: 16 (over z, x, core), blk: 2 (over y).
Axes of the slice: x: 2, y: 2, z: 4, core: 2. Of those that a mesh axis runs over, the one named last changes fastest.
Arguments:
- spectra: bfloat16 [1024, 2, 4, 512], P(('grp', 'blk')), may hold values from -6 to 6
- ownership: int32 [16, 2], replicated, may hold values from 0 to 1, each once within a row
- pairing: int32 [16], replicated, may hold values from 0 to 15, as said below
Outputs:
- near_corr: bfloat16 [1024, 64, 128], P(('grp', 'blk'))
- far_corr: bfloat16 [1024, 64, 128], P(('grp', 'blk'))
The draws below stay inside these ranges and needn't reach their ends.
Inputs may be any that keep to these rules, and one draw needn't show every extreme that they name: pairing[g] = g XOR m for all g, with one m of 1 to 15 for the round; so each group is its partner's partner and never its own.
All inputs are finite; a program needn't handle non-finite values.
Results may differ from the reference program's by a relative error of at most 0.0055.
Values may be sent and summed in bfloat16 or wider, within the bound.
A program may use at most 128 MiB of HBM per device.

```python
import jax
import jax.numpy as jnp
from jax import lax

F = 512
LAGS = 128
W = 4
CH_DEV = 32
CH_GRP = 64
CHANNELS = 1024
N_GRP = 16
N_BLK = 2


def draw_pairing(key, part):
    key = jax.random.fold_in(key, 7)
    offset = jax.random.randint(key, (), 1, N_GRP).astype(jnp.int32)
    return jnp.bitwise_xor(jnp.arange(N_GRP, dtype=jnp.int32), offset)


def level_of(own_key, extent, shards, least, top_value):
    level = 1.0
    for dim, blocks in shards:
        heights = jax.random.uniform(jax.random.fold_in(jax.random.fold_in(own_key, 6), dim), (blocks,), jnp.float32, least / len(shards), top_value / len(shards))
        level = level * jnp.repeat(jnp.exp(heights), extent[dim] // blocks).reshape((-1,) + (1,) * (len(extent) - 1 - dim))
    return level


def normal_values(rng, extent, scale, reach, cuts=(), kind=jnp.bfloat16):
    gain = level_of(rng, extent, cuts, -0.22, 0.18) if cuts else 1.0
    values = jax.random.normal(rng, extent, jnp.float32) * scale * gain
    return jnp.minimum(jnp.maximum(values, -reach), reach).astype(kind)


def setup_inputs(seed: int = 0) -> dict:
    arg_keys = jax.random.split(jax.random.key(seed), 4)
    return {
        "spectra": normal_values(arg_keys[0], (CHANNELS, 2, W, F), 1.0, 6.0, ((0, 32),)),
        "ownership": jax.vmap(lambda own: jax.random.permutation(own, N_BLK))(jax.random.split(arg_keys[1], N_GRP)).reshape((N_GRP, N_BLK)).astype(jnp.int32),
        "pairing": draw_pairing(jax.random.fold_in(arg_keys[3], 71), 0),
    }


def make_twiddle(freq_count, lag_count):
    freqs = jnp.arange(freq_count, dtype=jnp.int32)[:, None]
    shifts = jnp.arange(lag_count, dtype=jnp.int32)[None, :] - lag_count // 2
    phase = jnp.mod(freqs * shifts, 2 * freq_count).astype(jnp.float32)
    angle = jnp.float32(jnp.pi) * phase / jnp.float32(freq_count)
    return jnp.stack([jnp.cos(angle), -jnp.sin(angle)], 0).astype(jnp.bfloat16)

def correlate(own_rows, other_rows, twiddle):
    row_count = own_rows.shape[0]
    col_count = other_rows.shape[0]
    real_part = own_rows[:, 0].astype(jnp.float32)
    imag_part = own_rows[:, 1].astype(jnp.float32)
    first = jnp.concatenate([real_part, imag_part], 1)
    second = jnp.concatenate([imag_part, -real_part], 1)
    left_side = jnp.concatenate([first, second], 0)
    right_side = jnp.concatenate([other_rows[:, 0], other_rows[:, 1]], 1).astype(jnp.float32)
    cross = lax.dot_general(left_side, right_side, (((1,), (1,)), ((2,), (2,))), precision=lax.Precision.HIGHEST, preferred_element_type=jnp.float32)
    cross = (cross * jnp.float32(1.0 / W)).astype(jnp.bfloat16)
    cross = cross.reshape(cross.shape[0], 2, row_count, col_count).astype(jnp.float32)
    result = lax.dot_general(cross, twiddle.astype(jnp.float32), (((0, 1), (1, 0)), ((), ())), precision=lax.Precision.HIGHEST, preferred_element_type=jnp.float32)
    scale = jnp.float32(1.0) / jnp.sqrt(jnp.float32(F))
    return (result * scale).astype(jnp.bfloat16)

def reference(spectra, ownership, pairing):
    twiddle = make_twiddle(F, LAGS)
    blocked = spectra.reshape(N_GRP, N_BLK, CH_DEV, 2, W, F)
    inverse = jnp.argsort(ownership, axis=1).astype(jnp.int32)
    ordered = jnp.take_along_axis(blocked, inverse[:, :, None, None, None, None], axis=1)
    ordered = ordered.reshape(N_GRP, CH_GRP, 2, W, F)
    stored = blocked.reshape(N_GRP, CH_GRP, 2, W, F)

    def one_group(group_index):
        own_rows = stored[group_index]
        near_part = correlate(own_rows, ordered[group_index], twiddle)
        far_part = correlate(own_rows, ordered[pairing[group_index]], twiddle)
        return (near_part, far_part)
    near_corr, far_corr = lax.map(one_group, jnp.arange(N_GRP, dtype=jnp.int32))
    return (near_corr.reshape(CHANNELS, CH_GRP, LAGS), far_corr.reshape(CHANNELS, CH_GRP, LAGS))
```

```python
import functools

import jax
import jax.numpy as jnp
import numpy as np
from jax import lax
from jax.experimental import pallas as pl
from jax.experimental.pallas import tpu as pltpu
from jax.sharding import PartitionSpec as P

LAGS = 128
CHUNKS = 4
MESH = pl.DeviceIdType.MESH


def make_twiddle(freq_count, lag_count):
    freqs = np.arange(freq_count, dtype=np.int64)[:, None]
    shifts = np.arange(lag_count, dtype=np.int64)[None, :] - lag_count // 2
    phase = np.mod(freqs * shifts, 2 * freq_count).astype(np.float32)
    angle = np.float32(np.pi) * phase / np.float32(freq_count)
    return np.concatenate([np.cos(angle), -np.sin(angle)], 0).astype(jnp.bfloat16)


def flip(index, mask):
    bit = 1
    while bit <= mask:
        if mask & bit:
            index = index + bit - 2 * bit * ((index // bit) % 2)
        bit *= 2
    return index


def exchange_kernel(mask, block_count, x_ref, buf, far_send, far_recv, near_send, near_recv, fwd_send, fwd_recv, own_sem):
    group = lax.axis_index("grp")
    block = lax.axis_index("blk")
    partner = flip(group, mask)
    peers = [lax.rem(block + step, block_count) for step in range(block_count)]

    barrier = pltpu.get_barrier_semaphore()
    pl.semaphore_signal(barrier, inc=1, device_id=(partner, block), device_id_type=MESH)
    for step in range(1, block_count):
        pl.semaphore_signal(barrier, inc=1, device_id=(group, peers[step]), device_id_type=MESH)
    pl.semaphore_wait(barrier, block_count)

    part = x_ref.shape[0] // CHUNKS
    far = []
    for c in range(CHUNKS):
        rows = pl.ds(c * part, part)
        copy = pltpu.make_async_remote_copy(
            src_ref=x_ref.at[rows], dst_ref=buf.at[block_count, rows],
            send_sem=far_send.at[c], recv_sem=far_recv.at[c],
            device_id=(partner, block), device_id_type=MESH)
        copy.start()
        far.append(copy)
    near = []
    for step in range(1, block_count):
        copy = pltpu.make_async_remote_copy(
            src_ref=x_ref, dst_ref=buf.at[step],
            send_sem=near_send.at[step - 1], recv_sem=near_recv.at[step - 1],
            device_id=(group, peers[step]), device_id_type=MESH)
        copy.start()
        near.append(copy)
    own = pltpu.make_async_copy(x_ref, buf.at[0], own_sem)
    own.start()
    forward = []
    for c in range(CHUNKS):
        rows = pl.ds(c * part, part)
        far[c].wait_recv()
        for step in range(1, block_count):
            copy = pltpu.make_async_remote_copy(
                src_ref=buf.at[block_count, rows], dst_ref=buf.at[block_count + step, rows],
                send_sem=fwd_send.at[(step - 1) * CHUNKS + c], recv_sem=fwd_recv.at[(step - 1) * CHUNKS + c],
                device_id=(group, peers[step]), device_id_type=MESH)
            copy.start()
            forward.append(copy)
    own.wait()
    for copy in far:
        copy.wait_send()
    for copy in near + forward:
        copy.wait()


def exchange(mask, block_count, x):
    others = block_count - 1
    return pl.pallas_call(
        functools.partial(exchange_kernel, mask, block_count),
        out_shape=jax.ShapeDtypeStruct((2 * block_count,) + x.shape, x.dtype),
        in_specs=[pl.BlockSpec(memory_space=pltpu.VMEM)],
        out_specs=pl.BlockSpec(memory_space=pl.ANY),
        scratch_shapes=[
            pltpu.SemaphoreType.DMA((CHUNKS,)),
            pltpu.SemaphoreType.DMA((CHUNKS,)),
            pltpu.SemaphoreType.DMA((others,)),
            pltpu.SemaphoreType.DMA((others,)),
            pltpu.SemaphoreType.DMA((others * CHUNKS,)),
            pltpu.SemaphoreType.DMA((others * CHUNKS,)),
            pltpu.SemaphoreType.DMA,
        ],
        compiler_params=pltpu.CompilerParams(collective_id=mask, has_side_effects=True),
        name="exchange",
    )(x)


def tree_sum(terms):
    while len(terms) > 1:
        terms = [a + b for a, b in zip(terms[::2], terms[1::2])] + terms[len(terms) & ~1:]
    return terms[0]


def spread_rows(x_ref, wide):
    plane_count, row_count, freq_count = x_ref.shape

    def plane(k, carry):
        rows = x_ref[k].astype(jnp.float32)
        for r in range(row_count):
            wide[r, k] = jnp.broadcast_to(rows[r:r + 1], (16, freq_count)).astype(jnp.bfloat16)
        return carry

    lax.fori_loop(0, plane_count, plane, 0)


def cross_block(wide, y_ref, cross):
    row_count, plane_count = wide.shape[:2]
    window_count = plane_count // 2
    col_count, freq_count = y_ref.shape[1:]

    def row(r, carry):
        for f in range(0, freq_count, 128):
            lanes = slice(f, f + 128)
            x = [wide[r, k, :, lanes] for k in range(plane_count)]
            for j in range(0, col_count, 16):
                y = [y_ref[k, j:j + 16, lanes] for k in range(plane_count)]
                real, imag = [], []
                for w in range(window_count):
                    real.append(x[w] * y[w] + x[window_count + w] * y[window_count + w])
                    imag.append(x[window_count + w] * y[w] - x[w] * y[window_count + w])
                where = pl.ds(pl.multiple_of(r * col_count + j, 16), 16)
                cross[where, lanes] = tree_sum(real)
                cross[where, slice(freq_count + f, freq_count + f + 128)] = tree_sum(imag)
        return carry

    lax.fori_loop(0, row_count, row, 0)


def correlate_kernel(block_count, slots, twiddle_ref, x_ref, buf, near_ref, far_ref, wide, cross):
    row_count, col_count, freq_count = x_ref.shape[1], x_ref.shape[1], x_ref.shape[2]
    window_count = x_ref.shape[0] // 2
    scale = float(1.0 / (window_count * np.sqrt(np.float64(freq_count))))
    spread_rows(x_ref, wide)
    tile = 16
    for side, out in ((0, near_ref), (1, far_ref)):
        def block(step, carry):
            slot = side * block_count + step
            cross_block(wide, buf.at[slot], cross)
            place = pl.multiple_of(slots[slot] * col_count, col_count)

            def rows(i, inner):
                values = cross[pl.ds(pl.multiple_of(i * (tile * col_count), tile * col_count), tile * col_count)]
                result = jnp.dot(values, twiddle_ref[...], preferred_element_type=jnp.float32)
                result = (result * scale).astype(jnp.bfloat16).reshape(tile, col_count, -1)
                out[pl.ds(i * tile, tile), pl.ds(place, col_count), :] = result
                return inner

            lax.fori_loop(0, row_count // tile, rows, 0)
            return carry

        lax.fori_loop(0, block_count, block, 0)


def correlate(block_count, slots, twiddle, x, buf):
    plane_count, row_count, freq_count = x.shape
    lag_count = twiddle.shape[1]
    out = jax.ShapeDtypeStruct((row_count, block_count * row_count, lag_count), jnp.bfloat16)
    vmem = pl.BlockSpec(memory_space=pltpu.VMEM)
    return pl.pallas_call(
        functools.partial(correlate_kernel, block_count),
        out_shape=(out, out),
        in_specs=[pl.BlockSpec(memory_space=pltpu.SMEM), vmem, vmem, vmem],
        out_specs=(vmem, vmem),
        scratch_shapes=[
            pltpu.VMEM((row_count, plane_count, 16, freq_count), jnp.bfloat16),
            pltpu.VMEM((row_count * row_count, 2 * freq_count), jnp.bfloat16),
        ],
        compiler_params=pltpu.CompilerParams(vmem_limit_bytes=48 * 1024 * 1024),
        name="correlate",
    )(slots, twiddle, x, buf)


def shards(group_count, block_count, spectra, ownership, pairing):
    row_count, parts, window_count, freq_count = spectra.shape
    twiddle = jnp.asarray(make_twiddle(freq_count, LAGS))
    x = spectra.transpose(1, 2, 0, 3).reshape(parts * window_count, row_count, freq_count)
    group_index = lax.axis_index("grp")
    block_index = lax.axis_index("blk")
    stored = jnp.mod(block_index - jnp.arange(block_count, dtype=jnp.int32), block_count)
    slots = jnp.concatenate([ownership[group_index][stored], ownership[pairing[group_index]][stored]])
    branches = [functools.partial(exchange, mask, block_count) for mask in range(1, group_count)]
    buf = lax.switch(pairing[0] - 1, branches, x)
    return correlate(block_count, slots, twiddle, x, buf)


def solution(mesh):
    in_specs = (P(("grp", "blk"), None, None, None), P(), P())
    out_specs = (P(("grp", "blk"), None, None), P(("grp", "blk"), None, None))
    body = functools.partial(shards, mesh.shape["grp"], mesh.shape["blk"])
    return jax.shard_map(body, mesh=mesh, in_specs=in_specs, out_specs=out_specs, check_vma=False)
```

```python
import functools

import jax
import jax.numpy as jnp
import numpy as np
from jax import lax
from jax.experimental import pallas as pl
from jax.experimental.pallas import tpu as pltpu
from jax.sharding import PartitionSpec as P

LAGS = 128
CHUNKS = 2
MESH = pl.DeviceIdType.MESH


def make_twiddle(freq_count, lag_count):
    freqs = np.arange(freq_count, dtype=np.int64)[:, None]
    shifts = np.arange(lag_count, dtype=np.int64)[None, :] - lag_count // 2
    phase = np.mod(freqs * shifts, 2 * freq_count).astype(np.float32)
    angle = np.float32(np.pi) * phase / np.float32(freq_count)
    return np.concatenate([np.cos(angle), -np.sin(angle)], 0).astype(jnp.bfloat16)


def flip(index, mask):
    bit = 1
    while bit <= mask:
        if mask & bit:
            index = index + bit - 2 * bit * ((index // bit) % 2)
        bit *= 2
    return index


def tree_sum(terms):
    while len(terms) > 1:
        terms = [a + b for a, b in zip(terms[::2], terms[1::2])] + terms[len(terms) & ~1:]
    return terms[0]


def spread_rows(x_ref, wide):
    half_count, plane_count, row_count, freq_count = x_ref.shape

    def plane(k, carry):
        for h in range(half_count):
            rows = x_ref[h, k].astype(jnp.float32)
            for r in range(row_count):
                wide[h * row_count + r, k] = jnp.broadcast_to(
                    rows[r:r + 1], (row_count, freq_count)).astype(jnp.bfloat16)
        return carry

    lax.fori_loop(0, plane_count, plane, 0)


def cross_half(wide, y_ref, cross):
    row_count, plane_count = wide.shape[:2]
    windows = plane_count // 2
    col_count, freq_count = y_ref.shape[1:]
    for f in range(0, freq_count, 256):
        y = [y_ref[k, :, f:f + 256] for k in range(plane_count)]

        def row(r, carry):
            x = [wide[r, k, :, f:f + 256] for k in range(plane_count)]
            real, imag = [], []
            for w in range(windows):
                real.append(x[w] * y[w] + x[windows + w] * y[windows + w])
                imag.append(x[windows + w] * y[w] - x[w] * y[windows + w])
            where = pl.ds(pl.multiple_of(r * col_count, col_count), col_count)
            cross[where, f:f + 256] = tree_sum(real)
            cross[where, freq_count + f:freq_count + f + 256] = tree_sum(imag)
            return carry

        lax.fori_loop(0, row_count, row, 0, unroll=2)


def main_kernel(mask, block_count, x_ref, twiddle_ref, res_ref, buf, wide, cross, far_send, far_recv,
                near_send, near_recv, fwd_send, fwd_recv, own_sem):
    group = lax.axis_index("grp")
    block = lax.axis_index("blk")
    partner = flip(group, mask)
    peers = [lax.rem(block + step, block_count) for step in range(block_count)]
    plane_count, col_count, freq_count = x_ref.shape[1:]
    part = plane_count // CHUNKS

    def far_copy(h, c):
        planes = pl.ds(c * part, part)
        return pltpu.make_async_remote_copy(
            src_ref=x_ref.at[h, planes], dst_ref=buf.at[block_count, h, planes],
            send_sem=far_send.at[h, c], recv_sem=far_recv.at[h, c],
            device_id=(partner, block), device_id_type=MESH)

    def near_copy(step, h, peer):
        return pltpu.make_async_remote_copy(
            src_ref=x_ref.at[h], dst_ref=buf.at[step, h],
            send_sem=near_send.at[step - 1, h], recv_sem=near_recv.at[step - 1, h],
            device_id=(group, peer), device_id_type=MESH)

    def fwd_copy(step, h, c, peer):
        planes = pl.ds(c * part, part)
        return pltpu.make_async_remote_copy(
            src_ref=buf.at[block_count, h, planes], dst_ref=buf.at[block_count + step, h, planes],
            send_sem=fwd_send.at[step - 1, h, c], recv_sem=fwd_recv.at[step - 1, h, c],
            device_id=(group, peer), device_id_type=MESH)

    def pass_on(h, c):
        far_copy(h, c).wait_recv()
        for step in range(1, block_count):
            fwd_copy(step, h, c, peers[step]).start()

    barrier = pltpu.get_barrier_semaphore()
    pl.semaphore_signal(barrier, inc=1, device_id=(partner, block), device_id_type=MESH)
    for step in range(1, block_count):
        pl.semaphore_signal(barrier, inc=1, device_id=(group, peers[step]), device_id_type=MESH)
    own = pltpu.make_async_copy(x_ref, buf.at[0], own_sem)
    own.start()
    pl.semaphore_wait(barrier, block_count)
    for h in range(2):
        for c in range(CHUNKS):
            far_copy(h, c).start()
    for step in range(1, block_count):
        for h in range(2):
            near_copy(step, h, peers[step]).start()
    spread_rows(x_ref, wide)
    own.wait()

    scale = float(1.0 / (plane_count // 2 * np.sqrt(np.float64(freq_count))))
    tile = 16

    def unit(s, carry):
        slot, h = s // 2, s % 2

        @pl.when(s == 2)
        def _():
            for c in range(CHUNKS):
                pass_on(0, c)

        @pl.when((s >= 2) & (s < 2 * block_count))
        def _():
            near_copy(slot, h, peers[1]).wait_recv()

        for c in range(CHUNKS):
            @pl.when(s == 2 * block_count + c * 2 // CHUNKS)
            def _():
                pass_on(1, c)

        @pl.when(s >= 2 * block_count + 2)
        def _():
            for c in range(CHUNKS):
                fwd_copy(slot - block_count, h, c, peers[1]).wait_recv()

        cross_half(wide, buf.at[slot, h], cross)

        def rows(i, inner):
            here = pl.ds(pl.multiple_of(i * (tile * col_count), tile * col_count), tile * col_count)
            result = jnp.dot(cross[here], twiddle_ref[...], preferred_element_type=jnp.float32)
            result = (result * scale).astype(jnp.bfloat16).reshape(tile, col_count, -1)
            res_ref[slot, h, pl.ds(i * tile, tile)] = result
            return inner

        lax.fori_loop(0, wide.shape[0] // tile, rows, 0)
        return carry

    lax.fori_loop(0, 4 * block_count, unit, 0)

    for h in range(2):
        for c in range(CHUNKS):
            far_copy(h, c).wait_send()
            for step in range(1, block_count):
                fwd_copy(step, h, c, peers[step]).wait_send()
        for step in range(1, block_count):
            near_copy(step, h, peers[step]).wait_send()


def exchange_and_correlate(mask, block_count, x, twiddle):
    halves, plane_count, col_count, freq_count = x.shape
    row_count = halves * col_count
    others = block_count - 1
    vmem = pl.BlockSpec(memory_space=pltpu.VMEM)
    dma = pltpu.SemaphoreType.DMA
    return pl.pallas_call(
        functools.partial(main_kernel, mask, block_count),
        out_shape=jax.ShapeDtypeStruct(
            (2 * block_count, halves, row_count, col_count, twiddle.shape[1]), jnp.bfloat16),
        in_specs=[vmem, vmem],
        out_specs=vmem,
        scratch_shapes=[
            pltpu.VMEM((2 * block_count,) + x.shape, x.dtype),
            pltpu.VMEM((row_count, plane_count, col_count, freq_count), jnp.bfloat16),
            pltpu.VMEM((row_count * col_count, 2 * freq_count), jnp.bfloat16),
            dma((halves, CHUNKS)), dma((halves, CHUNKS)),
            dma((others, halves)), dma((others, halves)),
            dma((others, halves, CHUNKS)), dma((others, halves, CHUNKS)),
            dma,
        ],
        compiler_params=pltpu.CompilerParams(
            collective_id=mask, has_side_effects=True, vmem_limit_bytes=40 * 1024 * 1024),
        name="exchange_and_correlate",
    )(x, twiddle)


def order_kernel(group_count, block_count, ownership, pairing, res, near, far, sems):
    group = lax.axis_index("grp")
    block = lax.axis_index("blk")
    halves, col_count = res.shape[1], res.shape[3]
    copies = []
    for side, out, whose in ((0, near, group), (1, far, pairing[group])):
        for step in range(block_count):
            stored = lax.rem(block - step + block_count, block_count)
            channel = ownership[whose * block_count + stored]
            for h in range(halves):
                place = pl.multiple_of((channel * halves + h) * col_count, col_count)
                slot = side * block_count + step
                copy = pltpu.make_async_copy(
                    res.at[slot, h], out.at[:, pl.ds(place, col_count), :], sems.at[slot * halves + h])
                copy.start()
                copies.append(copy)
    for copy in copies:
        copy.wait()


def order(group_count, block_count, ownership, pairing, res):
    slots, halves, row_count, col_count, lag_count = res.shape
    out = jax.ShapeDtypeStruct((row_count, block_count * halves * col_count, lag_count), res.dtype)
    smem = pl.BlockSpec(memory_space=pltpu.SMEM)
    anywhere = pl.BlockSpec(memory_space=pl.ANY)
    return pl.pallas_call(
        functools.partial(order_kernel, group_count, block_count),
        out_shape=(out, out),
        in_specs=[smem, smem, anywhere],
        out_specs=(anywhere, anywhere),
        scratch_shapes=[pltpu.SemaphoreType.DMA((slots * halves,))],
        name="order",
    )(ownership, pairing, res)


def shards(group_count, block_count, spectra, ownership, pairing):
    row_count, parts, window_count, freq_count = spectra.shape
    twiddle = jnp.asarray(make_twiddle(freq_count, LAGS))
    x = spectra.reshape(2, row_count // 2, parts * window_count, freq_count).transpose(0, 2, 1, 3)
    branches = [functools.partial(exchange_and_correlate, mask, block_count) for mask in range(1, group_count)]
    res = lax.switch(pairing[0] - 1, branches, x, twiddle)
    return order(group_count, block_count, ownership.reshape(-1), pairing, res)


def solution(mesh):
    in_specs = (P(("grp", "blk"), None, None, None), P(), P())
    out_specs = (P(("grp", "blk"), None, None), P(("grp", "blk"), None, None))
    body = functools.partial(shards, mesh.shape["grp"], mesh.shape["blk"])
    return jax.shard_map(body, mesh=mesh, in_specs=in_specs, out_specs=out_specs, check_vma=False)
```

```python
import functools

import jax
import jax.numpy as jnp
import numpy as np
from jax import lax
from jax.experimental import pallas as pl
from jax.experimental.pallas import tpu as pltpu
from jax.sharding import PartitionSpec as P

LAGS = 128
CHUNKS = 2
MESH = pl.DeviceIdType.MESH


def make_twiddle(freq_count, lag_count):
    freqs = np.arange(freq_count, dtype=np.int64)[:, None]
    shifts = np.arange(lag_count, dtype=np.int64)[None, :] - lag_count // 2
    phase = np.mod(freqs * shifts, 2 * freq_count).astype(np.float32)
    angle = np.float32(np.pi) * phase / np.float32(freq_count)
    return np.concatenate([np.cos(angle), -np.sin(angle)], 0).astype(jnp.bfloat16)


def flip(index, mask):
    bit = 1
    while bit <= mask:
        if mask & bit:
            index = index + bit - 2 * bit * ((index // bit) % 2)
        bit *= 2
    return index


def tree_sum(terms):
    while len(terms) > 1:
        terms = [a + b for a, b in zip(terms[::2], terms[1::2])] + terms[len(terms) & ~1:]
    return terms[0]


def spread_rows(x_ref, wide):
    half_count, plane_count, row_count, freq_count = x_ref.shape

    def plane(k, carry):
        for h in range(half_count):
            rows = x_ref[h, k].astype(jnp.float32)
            for r in range(row_count):
                wide[h * row_count + r, k] = jnp.broadcast_to(
                    rows[r:r + 1], (row_count, freq_count)).astype(jnp.bfloat16)
        return carry

    lax.fori_loop(0, plane_count, plane, 0)


def cross_half(wide, y_ref, cross):
    row_count, plane_count = wide.shape[:2]
    windows = plane_count // 2
    col_count, freq_count = y_ref.shape[1:]
    for f in range(0, freq_count, 256):
        y = [y_ref[k, :, f:f + 256] for k in range(plane_count)]

        def row(r, carry):
            x = [wide[r, k, :, f:f + 256] for k in range(plane_count)]
            real, imag = [], []
            for w in range(windows):
                real.append(x[w] * y[w] + x[windows + w] * y[windows + w])
                imag.append(x[windows + w] * y[w] - x[w] * y[windows + w])
            where = pl.ds(pl.multiple_of(r * col_count, col_count), col_count)
            cross[where, f:f + 256] = tree_sum(real)
            cross[where, freq_count + f:freq_count + f + 256] = tree_sum(imag)
            return carry

        lax.fori_loop(0, row_count, row, 0, unroll=2)


def main_kernel(mask, block_count, x_ref, twiddle_ref, res_ref, buf, wide, cross, far_send, far_recv,
                near_send, near_recv, fwd_send, fwd_recv, own_sem):
    group = lax.axis_index("grp")
    block = lax.axis_index("blk")
    partner = flip(group, mask)
    peers = [lax.rem(block + step, block_count) for step in range(block_count)]
    plane_count, col_count, freq_count = x_ref.shape[1:]
    part = plane_count // CHUNKS

    def far_copy(h, c):
        planes = pl.ds(c * part, part)
        return pltpu.make_async_remote_copy(
            src_ref=x_ref.at[h, planes], dst_ref=buf.at[block_count, h, planes],
            send_sem=far_send.at[h, c], recv_sem=far_recv.at[h, c],
            device_id=(partner, block), device_id_type=MESH)

    def near_copy(step, h, peer):
        return pltpu.make_async_remote_copy(
            src_ref=x_ref.at[h], dst_ref=buf.at[step, h],
            send_sem=near_send.at[step - 1, h], recv_sem=near_recv.at[step - 1, h],
            device_id=(group, peer), device_id_type=MESH)

    def fwd_copy(step, h, c, peer):
        planes = pl.ds(c * part, part)
        return pltpu.make_async_remote_copy(
            src_ref=buf.at[block_count, h, planes], dst_ref=buf.at[block_count + step, h, planes],
            send_sem=fwd_send.at[step - 1, h, c], recv_sem=fwd_recv.at[step - 1, h, c],
            device_id=(group, peer), device_id_type=MESH)

    def pass_on(h, c):
        far_copy(h, c).wait_recv()
        for step in range(1, block_count):
            fwd_copy(step, h, c, peers[step]).start()

    barrier = pltpu.get_barrier_semaphore()
    pl.semaphore_signal(barrier, inc=1, device_id=(partner, block), device_id_type=MESH)
    for step in range(1, block_count):
        pl.semaphore_signal(barrier, inc=1, device_id=(group, peers[step]), device_id_type=MESH)
    own = pltpu.make_async_copy(x_ref, buf.at[0], own_sem)
    own.start()
    pl.semaphore_wait(barrier, block_count)
    for c in range(CHUNKS):
        far_copy(0, c).start()
    for h in range(2):
        for step in range(1, block_count):
            near_copy(step, h, peers[step]).start()
    spread_rows(x_ref, wide)
    own.wait()

    scale = float(1.0 / (plane_count // 2 * np.sqrt(np.float64(freq_count))))

    def unit(s, carry):
        q = s - 2 * block_count
        is_near = s < 2 * block_count
        slot = jnp.where(is_near, s // 2, block_count + q % block_count)
        h = jnp.where(is_near, s % 2, q // block_count)

        @pl.when(s == 3)
        def _():
            for c in range(CHUNKS):
                pass_on(0, c)
            for c in range(CHUNKS):
                far_copy(0, c).wait_send()
            far_copy(1, 0).start()

        @pl.when((s >= 2) & is_near)
        def _():
            near_copy(slot, h, peers[1]).wait_recv()

        @pl.when(q == 1)
        def _():
            pass_on(1, 0)
            far_copy(1, 0).wait_send()
            far_copy(1, 1).start()

        @pl.when(q == block_count)
        def _():
            pass_on(1, 1)

        @pl.when((q > 0) & (slot > block_count))
        def _():
            for c in range(CHUNKS):
                fwd_copy(slot - block_count, h, c, peers[1]).wait_recv()

        cross_half(wide, buf.at[slot, h], cross)

        result = jnp.dot(cross[...], twiddle_ref[...], preferred_element_type=jnp.float32)
        res_ref[slot, h] = (result * scale).astype(jnp.bfloat16).reshape(res_ref.shape[2:])
        return carry

    lax.fori_loop(0, 4 * block_count, unit, 0)

    far_copy(1, 1).wait_send()
    for h in range(2):
        for c in range(CHUNKS):
            for step in range(1, block_count):
                fwd_copy(step, h, c, peers[step]).wait_send()
        for step in range(1, block_count):
            near_copy(step, h, peers[step]).wait_send()


def exchange_and_correlate(mask, block_count, x, twiddle):
    halves, plane_count, col_count, freq_count = x.shape
    row_count = halves * col_count
    others = block_count - 1
    vmem = pl.BlockSpec(memory_space=pltpu.VMEM)
    dma = pltpu.SemaphoreType.DMA
    return pl.pallas_call(
        functools.partial(main_kernel, mask, block_count),
        out_shape=jax.ShapeDtypeStruct(
            (2 * block_count, halves, row_count, col_count, twiddle.shape[1]), jnp.bfloat16),
        in_specs=[vmem, vmem],
        out_specs=vmem,
        scratch_shapes=[
            pltpu.VMEM((2 * block_count,) + x.shape, x.dtype),
            pltpu.VMEM((row_count, plane_count, col_count, freq_count), jnp.bfloat16),
            pltpu.VMEM((row_count * col_count, 2 * freq_count), jnp.bfloat16),
            dma((halves, CHUNKS)), dma((halves, CHUNKS)),
            dma((others, halves)), dma((others, halves)),
            dma((others, halves, CHUNKS)), dma((others, halves, CHUNKS)),
            dma,
        ],
        compiler_params=pltpu.CompilerParams(
            collective_id=mask, has_side_effects=True, vmem_limit_bytes=40 * 1024 * 1024),
        name="exchange_and_correlate",
    )(x, twiddle)


def order_kernel(group_count, block_count, ownership, pairing, res, near, far, sems):
    group = lax.axis_index("grp")
    block = lax.axis_index("blk")
    halves, col_count = res.shape[1], res.shape[3]
    copies = []
    for side, out, whose in ((0, near, group), (1, far, pairing[group])):
        for step in range(block_count):
            stored = lax.rem(block - step + block_count, block_count)
            channel = ownership[stored, whose]
            for h in range(halves):
                place = pl.multiple_of((channel * halves + h) * col_count, col_count)
                slot = side * block_count + step
                copy = pltpu.make_async_copy(
                    res.at[slot, h], out.at[:, pl.ds(place, col_count), :], sems.at[slot * halves + h])
                copy.start()
                copies.append(copy)
    for copy in copies:
        copy.wait()


def order(group_count, block_count, ownership, pairing, res):
    slots, halves, row_count, col_count, lag_count = res.shape
    out = jax.ShapeDtypeStruct((row_count, block_count * halves * col_count, lag_count), res.dtype)
    smem = pl.BlockSpec(memory_space=pltpu.SMEM)
    anywhere = pl.BlockSpec(memory_space=pl.ANY)
    return pl.pallas_call(
        functools.partial(order_kernel, group_count, block_count),
        out_shape=(out, out),
        in_specs=[smem, smem, anywhere],
        out_specs=(anywhere, anywhere),
        scratch_shapes=[pltpu.SemaphoreType.DMA((slots * halves,))],
        name="order",
    )(ownership, pairing, res)


def shards(group_count, block_count, spectra, ownership, pairing):
    row_count, parts, window_count, freq_count = spectra.shape
    twiddle = jnp.asarray(make_twiddle(freq_count, LAGS))
    x = spectra.reshape(2, row_count // 2, parts * window_count, freq_count).transpose(0, 2, 1, 3)
    branches = [functools.partial(exchange_and_correlate, mask, block_count) for mask in range(1, group_count)]
    res = lax.switch(pairing[0] - 1, branches, x, twiddle)
    return order(group_count, block_count, ownership.T, pairing, res)


def solution(mesh):
    in_specs = (P(("grp", "blk"), None, None, None), P(), P())
    out_specs = (P(("grp", "blk"), None, None), P(("grp", "blk"), None, None))
    body = functools.partial(shards, mesh.shape["grp"], mesh.shape["blk"])
    return jax.shard_map(body, mesh=mesh, in_specs=in_specs, out_specs=out_specs, check_vma=False)
```

```python
import functools

import jax
import jax.numpy as jnp
import numpy as np
from jax import lax
from jax.experimental import pallas as pl
from jax.experimental.pallas import tpu as pltpu
from jax.sharding import PartitionSpec as P

LAGS = 128
CHUNKS = 2
ROWS = 8
MESH = pl.DeviceIdType.MESH


def make_twiddle(freq_count, lag_count):
    freqs = np.arange(freq_count, dtype=np.int64)[:, None]
    shifts = np.arange(lag_count, dtype=np.int64)[None, :] - lag_count // 2
    phase = np.mod(freqs * shifts, 2 * freq_count).astype(np.float32)
    angle = np.float32(np.pi) * phase / np.float32(freq_count)
    return np.concatenate([np.cos(angle), -np.sin(angle)], 0).astype(jnp.bfloat16)


def flip(index, mask):
    bit = 1
    while bit <= mask:
        if mask & bit:
            index = index + bit - 2 * bit * ((index // bit) % 2)
        bit *= 2
    return index


def tree_sum(terms):
    while len(terms) > 1:
        terms = [a + b for a, b in zip(terms[::2], terms[1::2])] + terms[len(terms) & ~1:]
    return terms[0]


def spread_rows(x_ref, wide):
    half_count, plane_count, row_count, freq_count = x_ref.shape

    def plane(k, carry):
        for h in range(half_count):
            rows = x_ref[h, k].astype(jnp.float32)
            for r in range(row_count):
                wide[h * row_count + r, k] = jnp.broadcast_to(
                    rows[r:r + 1], (row_count, freq_count)).astype(jnp.bfloat16)
        return carry

    lax.fori_loop(0, plane_count, plane, 0)


def cross_half(wide, y_ref, cross):
    row_count, plane_count = wide.shape[:2]
    windows = plane_count // 2
    col_count, freq_count = y_ref.shape[1:]
    for f in range(0, freq_count, 256):
        y = [y_ref[k, :, f:f + 256] for k in range(plane_count)]

        def rows(i, carry):
            for r in range(ROWS):
                x = [wide[i * ROWS + r, k, :, f:f + 256] for k in range(plane_count)]
                real, imag = [], []
                for w in range(windows):
                    real.append(x[w] * y[w] + x[windows + w] * y[windows + w])
                    imag.append(x[windows + w] * y[w] - x[w] * y[windows + w])
                where = pl.ds(pl.multiple_of((i * ROWS + r) * col_count, col_count), col_count)
                cross[where, f:f + 256] = tree_sum(real)
                cross[where, freq_count + f:freq_count + f + 256] = tree_sum(imag)
            return carry

        lax.fori_loop(0, row_count // ROWS, rows, 0)


def main_kernel(mask, block_count, x_ref, twiddle_ref, res_ref, buf, wide, cross, far_send, far_recv,
                near_send, near_recv, fwd_send, fwd_recv, own_sem):
    group = lax.axis_index("grp")
    block = lax.axis_index("blk")
    partner = flip(group, mask)
    peers = [lax.rem(block + step, block_count) for step in range(block_count)]
    plane_count, col_count, freq_count = x_ref.shape[1:]
    part = plane_count // CHUNKS

    def far_copy(h, c):
        planes = pl.ds(c * part, part)
        return pltpu.make_async_remote_copy(
            src_ref=x_ref.at[h, planes], dst_ref=buf.at[block_count, h, planes],
            send_sem=far_send.at[h, c], recv_sem=far_recv.at[h, c],
            device_id=(partner, block), device_id_type=MESH)

    def near_copy(step, h, peer):
        return pltpu.make_async_remote_copy(
            src_ref=x_ref.at[h], dst_ref=buf.at[step, h],
            send_sem=near_send.at[step - 1, h], recv_sem=near_recv.at[step - 1, h],
            device_id=(group, peer), device_id_type=MESH)

    def fwd_copy(step, h, c, peer):
        planes = pl.ds(c * part, part)
        return pltpu.make_async_remote_copy(
            src_ref=buf.at[block_count, h, planes], dst_ref=buf.at[block_count + step, h, planes],
            send_sem=fwd_send.at[step - 1, h, c], recv_sem=fwd_recv.at[step - 1, h, c],
            device_id=(group, peer), device_id_type=MESH)

    def pass_on(h, c):
        far_copy(h, c).wait_recv()
        for step in range(1, block_count):
            fwd_copy(step, h, c, peers[step]).start()

    barrier = pltpu.get_barrier_semaphore()
    pl.semaphore_signal(barrier, inc=1, device_id=(partner, block), device_id_type=MESH)
    for step in range(1, block_count):
        pl.semaphore_signal(barrier, inc=1, device_id=(group, peers[step]), device_id_type=MESH)
    own = pltpu.make_async_copy(x_ref, buf.at[0], own_sem)
    own.start()
    pl.semaphore_wait(barrier, block_count)
    for c in range(CHUNKS):
        far_copy(0, c).start()
    for h in range(2):
        for step in range(1, block_count):
            near_copy(step, h, peers[step]).start()
    spread_rows(x_ref, wide)
    own.wait()

    scale = float(1.0 / (plane_count // 2 * np.sqrt(np.float64(freq_count))))

    def unit(s, carry):
        q = s - 2 * block_count
        is_near = s < 2 * block_count
        slot = jnp.where(is_near, s // 2, block_count + q % block_count)
        h = jnp.where(is_near, s % 2, q // block_count)

        @pl.when(s == 3)
        def _():
            for c in range(CHUNKS):
                pass_on(0, c)
            for c in range(CHUNKS):
                far_copy(0, c).wait_send()
            far_copy(1, 0).start()

        @pl.when((s >= 2) & is_near)
        def _():
            near_copy(slot, h, peers[1]).wait_recv()

        @pl.when(q == 1)
        def _():
            pass_on(1, 0)
            far_copy(1, 0).wait_send()
            far_copy(1, 1).start()

        @pl.when(q == block_count)
        def _():
            pass_on(1, 1)

        @pl.when((q > 0) & (slot > block_count))
        def _():
            for c in range(CHUNKS):
                fwd_copy(slot - block_count, h, c, peers[1]).wait_recv()

        cross_half(wide, buf.at[slot, h], cross)

        result = jnp.dot(cross[...], twiddle_ref[...], preferred_element_type=jnp.float32)
        res_ref[slot, h] = (result * scale).astype(jnp.bfloat16).reshape(res_ref.shape[2:])
        return carry

    lax.fori_loop(0, 4 * block_count, unit, 0)

    far_copy(1, 1).wait_send()
    for h in range(2):
        for c in range(CHUNKS):
            for step in range(1, block_count):
                fwd_copy(step, h, c, peers[step]).wait_send()
        for step in range(1, block_count):
            near_copy(step, h, peers[step]).wait_send()


def exchange_and_correlate(mask, block_count, x, twiddle):
    halves, plane_count, col_count, freq_count = x.shape
    row_count = halves * col_count
    others = block_count - 1
    vmem = pl.BlockSpec(memory_space=pltpu.VMEM)
    dma = pltpu.SemaphoreType.DMA
    return pl.pallas_call(
        functools.partial(main_kernel, mask, block_count),
        out_shape=jax.ShapeDtypeStruct(
            (2 * block_count, halves, row_count, col_count, twiddle.shape[1]), jnp.bfloat16),
        in_specs=[vmem, vmem],
        out_specs=vmem,
        scratch_shapes=[
            pltpu.VMEM((2 * block_count,) + x.shape, x.dtype),
            pltpu.VMEM((row_count, plane_count, col_count, freq_count), jnp.bfloat16),
            pltpu.VMEM((row_count * col_count, 2 * freq_count), jnp.bfloat16),
            dma((halves, CHUNKS)), dma((halves, CHUNKS)),
            dma((others, halves)), dma((others, halves)),
            dma((others, halves, CHUNKS)), dma((others, halves, CHUNKS)),
            dma,
        ],
        compiler_params=pltpu.CompilerParams(
            collective_id=mask, has_side_effects=True, vmem_limit_bytes=40 * 1024 * 1024),
        name="exchange_and_correlate",
    )(x, twiddle)


def order_kernel(group_count, block_count, ownership, pairing, res, near, far, sems):
    group = lax.axis_index("grp")
    block = lax.axis_index("blk")
    halves, col_count = res.shape[1], res.shape[3]
    copies = []
    for side, out, whose in ((0, near, group), (1, far, pairing[group])):
        for step in range(block_count):
            stored = lax.rem(block - step + block_count, block_count)
            channel = ownership[stored, whose]
            for h in range(halves):
                place = pl.multiple_of((channel * halves + h) * col_count, col_count)
                slot = side * block_count + step
                copy = pltpu.make_async_copy(
                    res.at[slot, h], out.at[:, pl.ds(place, col_count), :], sems.at[slot * halves + h])
                copy.start()
                copies.append(copy)
    for copy in copies:
        copy.wait()


def order(group_count, block_count, ownership, pairing, res):
    slots, halves, row_count, col_count, lag_count = res.shape
    out = jax.ShapeDtypeStruct((row_count, block_count * halves * col_count, lag_count), res.dtype)
    smem = pl.BlockSpec(memory_space=pltpu.SMEM)
    anywhere = pl.BlockSpec(memory_space=pl.ANY)
    return pl.pallas_call(
        functools.partial(order_kernel, group_count, block_count),
        out_shape=(out, out),
        in_specs=[smem, smem, anywhere],
        out_specs=(anywhere, anywhere),
        scratch_shapes=[pltpu.SemaphoreType.DMA((slots * halves,))],
        name="order",
    )(ownership, pairing, res)


def shards(group_count, block_count, spectra, ownership, pairing):
    row_count, parts, window_count, freq_count = spectra.shape
    twiddle = jnp.asarray(make_twiddle(freq_count, LAGS))
    x = spectra.reshape(2, row_count // 2, parts * window_count, freq_count).transpose(0, 2, 1, 3)
    branches = [functools.partial(exchange_and_correlate, mask, block_count) for mask in range(1, group_count)]
    res = lax.switch(pairing[0] - 1, branches, x, twiddle)
    return order(group_count, block_count, ownership.T, pairing, res)


def solution(mesh):
    in_specs = (P(("grp", "blk"), None, None, None), P(), P())
    out_specs = (P(("grp", "blk"), None, None), P(("grp", "blk"), None, None))
    body = functools.partial(shards, mesh.shape["grp"], mesh.shape["blk"])
    return jax.shard_map(body, mesh=mesh, in_specs=in_specs, out_specs=out_specs, check_vma=False)
```

```python
import functools

import jax
import jax.numpy as jnp
import numpy as np
from jax import lax
from jax.experimental import pallas as pl
from jax.experimental.pallas import tpu as pltpu
from jax.sharding import PartitionSpec as P

LAGS = 128
CHUNKS = 2
ROWS = 8
MESH = pl.DeviceIdType.MESH


def make_twiddle(freq_count, lag_count):
    freqs = np.arange(freq_count, dtype=np.int64)[:, None]
    shifts = np.arange(lag_count, dtype=np.int64)[None, :] - lag_count // 2
    phase = np.mod(freqs * shifts, 2 * freq_count).astype(np.float32)
    angle = np.float32(np.pi) * phase / np.float32(freq_count)
    return np.concatenate([np.cos(angle), -np.sin(angle)], 0).astype(jnp.bfloat16)


def flip(index, mask):
    bit = 1
    while bit <= mask:
        if mask & bit:
            index = index + bit - 2 * bit * ((index // bit) % 2)
        bit *= 2
    return index


def tree_sum(terms):
    while len(terms) > 1:
        terms = [a + b for a, b in zip(terms[::2], terms[1::2])] + terms[len(terms) & ~1:]
    return terms[0]


def spread_rows(x_ref, wide):
    half_count, plane_count, row_count, freq_count = x_ref.shape

    def plane(k, carry):
        for h in range(half_count):
            rows = x_ref[h, k].astype(jnp.float32)
            for r in range(row_count):
                wide[h * row_count + r, k] = jnp.broadcast_to(
                    rows[r:r + 1], (row_count, freq_count)).astype(jnp.bfloat16)
        return carry

    lax.fori_loop(0, plane_count, plane, 0)


def cross_half(wide, y_ref, cross):
    row_count, plane_count = wide.shape[:2]
    windows = plane_count // 2
    col_count, freq_count = y_ref.shape[1:]
    for f in range(0, freq_count, 256):
        y = [y_ref[k, :, f:f + 256] for k in range(plane_count)]

        def rows(i, carry):
            for r in range(ROWS):
                x = [wide[i * ROWS + r, k, :, f:f + 256] for k in range(plane_count)]
                real, imag = [], []
                for w in range(windows):
                    real.append(x[w] * y[w] + x[windows + w] * y[windows + w])
                    imag.append(x[windows + w] * y[w] - x[w] * y[windows + w])
                where = pl.ds(pl.multiple_of((i * ROWS + r) * col_count, col_count), col_count)
                cross[where, f:f + 256] = tree_sum(real)
                cross[where, freq_count + f:freq_count + f + 256] = tree_sum(imag)
            return carry

        lax.fori_loop(0, row_count // ROWS, rows, 0)


def main_kernel(mask, block_count, x_ref, twiddle_ref, res_ref, buf, wide, cross, far_send, far_recv,
                near_send, near_recv, fwd_send, fwd_recv, own_sem):
    group = lax.axis_index("grp")
    block = lax.axis_index("blk")
    partner = flip(group, mask)
    peers = [lax.rem(block + step, block_count) for step in range(block_count)]
    plane_count, col_count, freq_count = x_ref.shape[1:]
    part = plane_count // CHUNKS

    def far_copy(h, c):
        planes = pl.ds(c * part, part)
        return pltpu.make_async_remote_copy(
            src_ref=x_ref.at[h, planes], dst_ref=buf.at[block_count, h, planes],
            send_sem=far_send.at[h, c], recv_sem=far_recv.at[h, c],
            device_id=(partner, block), device_id_type=MESH)

    def near_copy(step, h, peer):
        return pltpu.make_async_remote_copy(
            src_ref=x_ref.at[h], dst_ref=buf.at[step, h],
            send_sem=near_send.at[step - 1, h], recv_sem=near_recv.at[step - 1, h],
            device_id=(group, peer), device_id_type=MESH)

    def fwd_copy(step, h, c, peer):
        planes = pl.ds(c * part, part)
        return pltpu.make_async_remote_copy(
            src_ref=buf.at[block_count, h, planes], dst_ref=buf.at[block_count + step, h, planes],
            send_sem=fwd_send.at[step - 1, h, c], recv_sem=fwd_recv.at[step - 1, h, c],
            device_id=(group, peer), device_id_type=MESH)

    def pass_on(h, c):
        far_copy(h, c).wait_recv()
        for step in range(1, block_count):
            fwd_copy(step, h, c, peers[step]).start()

    barrier = pltpu.get_barrier_semaphore()
    pl.semaphore_signal(barrier, inc=1, device_id=(partner, block), device_id_type=MESH)
    for step in range(1, block_count):
        pl.semaphore_signal(barrier, inc=1, device_id=(group, peers[step]), device_id_type=MESH)
    own = pltpu.make_async_copy(x_ref, buf.at[0], own_sem)
    own.start()
    pl.semaphore_wait(barrier, block_count)
    for h in range(2):
        for c in range(CHUNKS):
            far_copy(h, c).start()
    for h in range(2):
        for step in range(1, block_count):
            near_copy(step, h, peers[step]).start()
    spread_rows(x_ref, wide)
    own.wait()

    scale = float(1.0 / (plane_count // 2 * np.sqrt(np.float64(freq_count))))

    def unit(s, carry):
        q = s - 2 * block_count
        is_near = s < 2 * block_count
        slot = jnp.where(is_near, s // 2, block_count + q % block_count)
        h = jnp.where(is_near, s % 2, q // block_count)

        @pl.when(s == 3)
        def _():
            for c in range(CHUNKS):
                pass_on(0, c)

        @pl.when((s >= 2) & is_near)
        def _():
            near_copy(slot, h, peers[1]).wait_recv()

        @pl.when(q == 1)
        def _():
            pass_on(1, 0)

        @pl.when(q == block_count)
        def _():
            pass_on(1, 1)

        @pl.when((q > 0) & (slot > block_count))
        def _():
            for c in range(CHUNKS):
                fwd_copy(slot - block_count, h, c, peers[1]).wait_recv()

        cross_half(wide, buf.at[slot, h], cross)

        result = jnp.dot(cross[...], twiddle_ref[...], preferred_element_type=jnp.float32)
        res_ref[slot, h] = (result * scale).astype(jnp.bfloat16).reshape(res_ref.shape[2:])
        return carry

    lax.fori_loop(0, 4 * block_count, unit, 0)

    for h in range(2):
        for c in range(CHUNKS):
            far_copy(h, c).wait_send()
            for step in range(1, block_count):
                fwd_copy(step, h, c, peers[step]).wait_send()
        for step in range(1, block_count):
            near_copy(step, h, peers[step]).wait_send()


def exchange_and_correlate(mask, block_count, x, twiddle):
    halves, plane_count, col_count, freq_count = x.shape
    row_count = halves * col_count
    others = block_count - 1
    vmem = pl.BlockSpec(memory_space=pltpu.VMEM)
    dma = pltpu.SemaphoreType.DMA
    return pl.pallas_call(
        functools.partial(main_kernel, mask, block_count),
        out_shape=jax.ShapeDtypeStruct(
            (2 * block_count, halves, row_count, col_count, twiddle.shape[1]), jnp.bfloat16),
        in_specs=[vmem, vmem],
        out_specs=vmem,
        scratch_shapes=[
            pltpu.VMEM((2 * block_count,) + x.shape, x.dtype),
            pltpu.VMEM((row_count, plane_count, col_count, freq_count), jnp.bfloat16),
            pltpu.VMEM((row_count * col_count, 2 * freq_count), jnp.bfloat16),
            dma((halves, CHUNKS)), dma((halves, CHUNKS)),
            dma((others, halves)), dma((others, halves)),
            dma((others, halves, CHUNKS)), dma((others, halves, CHUNKS)),
            dma,
        ],
        compiler_params=pltpu.CompilerParams(
            collective_id=mask, has_side_effects=True, vmem_limit_bytes=40 * 1024 * 1024),
        name="exchange_and_correlate",
    )(x, twiddle)


def order_kernel(group_count, block_count, ownership, pairing, res, near, far, sems):
    group = lax.axis_index("grp")
    block = lax.axis_index("blk")
    halves, col_count = res.shape[1], res.shape[3]
    copies = []
    for side, out, whose in ((0, near, group), (1, far, pairing[group])):
        for step in range(block_count):
            stored = lax.rem(block - step + block_count, block_count)
            channel = ownership[stored, whose]
            for h in range(halves):
                place = pl.multiple_of((channel * halves + h) * col_count, col_count)
                slot = side * block_count + step
                copy = pltpu.make_async_copy(
                    res.at[slot, h], out.at[:, pl.ds(place, col_count), :], sems.at[slot * halves + h])
                copy.start()
                copies.append(copy)
    for copy in copies:
        copy.wait()


def order(group_count, block_count, ownership, pairing, res):
    slots, halves, row_count, col_count, lag_count = res.shape
    out = jax.ShapeDtypeStruct((row_count, block_count * halves * col_count, lag_count), res.dtype)
    smem = pl.BlockSpec(memory_space=pltpu.SMEM)
    anywhere = pl.BlockSpec(memory_space=pl.ANY)
    return pl.pallas_call(
        functools.partial(order_kernel, group_count, block_count),
        out_shape=(out, out),
        in_specs=[smem, smem, anywhere],
        out_specs=(anywhere, anywhere),
        scratch_shapes=[pltpu.SemaphoreType.DMA((slots * halves,))],
        name="order",
    )(ownership, pairing, res)


def shards(group_count, block_count, spectra, ownership, pairing):
    row_count, parts, window_count, freq_count = spectra.shape
    twiddle = jnp.asarray(make_twiddle(freq_count, LAGS))
    x = spectra.reshape(2, row_count // 2, parts * window_count, freq_count).transpose(0, 2, 1, 3)
    branches = [functools.partial(exchange_and_correlate, mask, block_count) for mask in range(1, group_count)]
    res = lax.switch(pairing[0] - 1, branches, x, twiddle)
    return order(group_count, block_count, ownership.T, pairing, res)


def solution(mesh):
    in_specs = (P(("grp", "blk"), None, None, None), P(), P())
    out_specs = (P(("grp", "blk"), None, None), P(("grp", "blk"), None, None))
    body = functools.partial(shards, mesh.shape["grp"], mesh.shape["blk"])
    return jax.shard_map(body, mesh=mesh, in_specs=in_specs, out_specs=out_specs, check_vma=False)
```
